32 devices in a mesh: sweep: 8 (over y, x, core), span: 4 (over z).
Axes of the slice: x: 2, y: 2, z: 4, core: 2. Of those that a mesh axis runs over, the one named last changes fastest.
Arguments:
- inverses: bfloat16 [8, 4, 6, 135, 135], P('sweep', 'span')
- couplings: bfloat16 [6, 8, 4, 6, 135, 135], P(None, 'sweep', 'span')
- rhs: bfloat16 [8, 4, 6, 135, 128], P('sweep', 'span'), may hold values from -6 to 6
- previous: bfloat16 [8, 4, 6, 135, 128], P('sweep', 'span'), may hold values from -6 to 6
- slot_layer: int32 [8, 4, 6], P('sweep', 'span'), may hold values from 0 to 5, each once within a row
Outputs:
- solution: float32 [8, 4, 6, 135, 128], P('sweep', 'span')
The draws below stay inside these ranges and needn't reach their ends.
Inputs may be any that keep to these rules, and one draw needn't show every extreme that they name: `slot_layer`: in each line each wall-normal layer is stored in exactly one slot.
All inputs are finite; a program needn't handle non-finite values.
Results may differ from the reference program's by a relative error of at most 0.0029.
Values may be sent and summed in bfloat16 or wider, within the bound.
A program may use at most 128 MiB of HBM per device.

```python
import math
import jax
import jax.numpy as jnp
from jax import lax

BS = 135
NRHS = 128
NZ = 6
NX = 8
NY = 4


def draw_inverses(key, part):
    shape = (NX, NY, NZ, BS, BS)
    noise = jax.random.normal(key, shape, jnp.float32)
    unit = jnp.eye(BS, dtype=jnp.float32)
    return (0.5 * (unit + 0.5 * noise / math.sqrt(BS))).astype(jnp.bfloat16)


def draw_couplings(key, part):
    shape = (6, NX, NY, NZ, BS, BS)
    noise = jnp.clip(jax.random.normal(key, shape, jnp.float32), -4.0, 4.0)
    face_scale = jnp.array([1.7, 1.0, 1.0, 1.0, 1.0, 1.0], jnp.float32).reshape(6, 1, 1, 1, 1, 1)
    return (noise * face_scale / math.sqrt(BS)).astype(jnp.bfloat16)


def block_scale(rng, extent, shards, least, top_value):
    level, own = 1.0, jax.random.fold_in(rng, 6)
    for dim, blocks in shards:
        draws = jnp.exp(jax.random.uniform(jax.random.fold_in(own, dim), (blocks,), jnp.float32, least / len(shards), top_value / len(shards)))
        level = level * jnp.repeat(draws, extent[dim] // blocks).reshape([-1 if axis == dim else 1 for axis in range(len(extent))])
    return level


def centred(own_key, shape, spread, most, split=(), kind=jnp.bfloat16):
    values = jax.random.normal(own_key, shape, jnp.float32) * spread
    if len(split) > 0:
        values = block_scale(own_key, shape, split, -0.22, 0.18) * values
    return jnp.clip(values, min=-most, max=most).astype(kind)


def setup_inputs(seed: int = 0) -> dict:
    streams_of = jax.random.split(jax.random.key(seed), 6)
    return {
        "inverses": draw_inverses(jax.random.fold_in(streams_of[5], 71), 0),
        "couplings": draw_couplings(jax.random.fold_in(streams_of[5], 71), 0),
        "rhs": centred(streams_of[2], (NX, NY, NZ, BS, NRHS), 1.0, 6.0, ((0, 8), (1, 4))),
        "previous": centred(streams_of[3], (NX, NY, NZ, BS, NRHS), 1.0, 6.0, ((0, 8), (1, 4))),
        "slot_layer": jax.vmap(lambda own: jax.random.permutation(own, NZ))(jax.random.split(streams_of[4], NX * NY)).reshape((NX, NY, NZ)).astype(jnp.int32),
    }


def couple(blocks, vectors):
    return jnp.einsum("...ab,...br->...ar", blocks.astype(jnp.float32), vectors.astype(jnp.float32), precision=lax.Precision.HIGHEST)


def select_layers(slot_layer, values, step_by):
    chooser = (slot_layer[:, :, None, :] == slot_layer[:, :, :, None] + step_by).astype(jnp.float32)
    picked = jnp.einsum("ijst,ijtbr->ijsbr", chooser, values.astype(jnp.float32), precision=lax.Precision.HIGHEST)
    return picked.astype(jnp.bfloat16)


def reference(inverses, couplings, rhs, previous, slot_layer):
    downstream = jnp.concatenate([previous[1:], jnp.zeros_like(previous[:1])], axis=0)
    span_lower = jnp.roll(previous, 1, axis=1)
    span_upper = jnp.roll(previous, -1, axis=1)
    wall_lower = select_layers(slot_layer, previous, -1)
    wall_upper = select_layers(slot_layer, previous, 1)
    coupled = couple(couplings[1], downstream)
    coupled = coupled + couple(couplings[2], span_lower)
    coupled = coupled + couple(couplings[3], span_upper)
    coupled = coupled + couple(couplings[4], wall_lower)
    coupled = coupled + couple(couplings[5], wall_upper)
    forcing = (rhs.astype(jnp.float32) - coupled).astype(jnp.bfloat16)
    offset = couple(inverses, forcing)
    transfer = -couple(inverses, couplings[0])

    def advance(inflow, pieces):
        matrix, shift_term = pieces
        fresh = shift_term + jnp.einsum("lzab,lzbr->lzar", matrix, inflow, precision=lax.Precision.HIGHEST)
        return fresh, fresh

    initial = jnp.zeros(offset.shape[1:], jnp.float32)
    unused, solution = lax.scan(advance, initial, (transfer, offset))
    return solution
```

```python
import functools

import jax
import jax.numpy as jnp
from jax import lax
from jax.experimental import pallas as pl
from jax.experimental.pallas import tpu as pltpu
from jax.sharding import PartitionSpec as P

MESH = pl.DeviceIdType.MESH


def split(value):
    high = value.astype(jnp.bfloat16)
    low = (value - high.astype(jnp.float32)).astype(jnp.bfloat16)
    return high, low


def mul(a, b):
    return jnp.dot(a, b, preferred_element_type=jnp.float32)


def kernel(
    planes, lines,
    layer, inv_hbm, coup_hbm, rhs_hbm, prev_hbm,
    out,
    inv, coup, rhs, prev, lower, upper, down, inflow, high, low, part,
    load_sem, halo_send, halo_recv, relay_send, relay_recv,
):
    slots = prev.shape[0]
    me = lax.axis_index("sweep")
    line = lax.axis_index("span")
    left = {"span": lax.rem(line + lines - 1, lines)}
    right = {"span": lax.rem(line + 1, lines)}
    up = {"sweep": jnp.maximum(me - 1, 0)}
    after = {"sweep": jnp.minimum(me + 1, planes - 1)}
    has_up = me > 0
    has_after = me < planes - 1

    pairs = [(prev_hbm, prev), (inv_hbm, inv), (rhs_hbm, rhs)]
    loads = [
        pltpu.make_async_copy(a, b, load_sem.at[k]) for k, (a, b) in enumerate(pairs)
    ]
    faces = [
        pltpu.make_async_copy(coup_hbm.at[f], coup.at[f], load_sem.at[len(pairs) + f])
        for f in range(6)
    ]
    for copy in (loads[1], faces[0], loads[0], faces[4], faces[5], loads[2]):
        copy.start()
    for copy in faces[1:4]:
        copy.start()

    barrier = pltpu.get_barrier_semaphore()
    pl.semaphore_signal(barrier, inc=1, device_id=left, device_id_type=MESH)
    pl.semaphore_signal(barrier, inc=1, device_id=right, device_id_type=MESH)

    @pl.when(has_up)
    def _():
        pl.semaphore_signal(barrier, inc=1, device_id=up, device_id_type=MESH)

    @pl.when(has_after)
    def _():
        pl.semaphore_signal(barrier, inc=1, device_id=after, device_id_type=MESH)

    expected = 2 + has_up.astype(jnp.int32) + has_after.astype(jnp.int32)
    pl.semaphore_wait(barrier, expected)

    def halo(kind, s):
        target, ref = ((right, lower), (left, upper), (up, down))[kind]
        return pltpu.make_async_remote_copy(
            src_ref=prev_hbm.at[s],
            dst_ref=ref.at[s],
            send_sem=halo_send.at[kind, s],
            recv_sem=halo_recv.at[kind, s],
            device_id=target,
            device_id_type=MESH,
        )

    def relay(s):
        return pltpu.make_async_remote_copy(
            src_ref=out.at[s],
            dst_ref=inflow.at[s],
            send_sem=relay_send.at[s],
            recv_sem=relay_recv.at[s],
            device_id=after,
            device_id_type=MESH,
        )

    for s in range(slots):
        halo(0, s).start()
        halo(1, s).start()

    @pl.when(has_up)
    def _():
        for s in range(slots):
            halo(2, s).start()

    @pl.when(jnp.logical_not(has_after))
    def _():
        down[...] = jnp.zeros_like(down)

    @pl.when(jnp.logical_not(has_up))
    def _():
        inflow[...] = jnp.zeros_like(inflow)

    loads[1].wait()
    faces[0].wait()
    for s in range(slots):
        transfer = -mul(inv[s], coup[0, s])
        high[s], low[s] = split(transfer)

    loads[0].wait()
    faces[4].wait()
    faces[5].wait()
    loads[2].wait()

    for s in range(slots):
        total = rhs[s].astype(jnp.float32)
        for face, step in ((4, -1), (5, 1)):
            wanted = layer[s] + step
            found = jnp.int32(0)
            known = jnp.int32(0)
            for t in range(slots):
                hit = (layer[t] == wanted).astype(jnp.int32)
                found = found + t * hit
                known = known + hit
            vector = prev[found].astype(jnp.float32) * known.astype(jnp.float32)
            total = total - mul(coup[face, s], vector.astype(jnp.bfloat16))
        part[s] = total

    for copy in faces[1:4]:
        copy.wait()

    for s in range(slots):
        halo(0, s).wait_recv()
        halo(1, s).wait_recv()

        @pl.when(has_after)
        def _():
            halo(2, s).wait_recv()

        coupled = mul(coup[1, s], down[s])
        coupled = coupled + mul(coup[2, s], lower[s])
        coupled = coupled + mul(coup[3, s], upper[s])
        forcing = (part[s] - coupled).astype(jnp.bfloat16)
        offset = mul(inv[s], forcing)

        @pl.when(has_up)
        def _():
            relay(s).wait_recv()

        first, second = split(inflow[s])
        both = mul(high[s], jnp.concatenate([first, second], axis=1))
        width = first.shape[1]
        rest = mul(low[s], first)
        out[s] = offset + (both[:, :width] + (both[:, width:] + rest))

        @pl.when(has_after)
        def _():
            relay(s).start()

    for s in range(slots):
        halo(0, s).wait_send()
        halo(1, s).wait_send()

    @pl.when(has_up)
    def _():
        for s in range(slots):
            halo(2, s).wait_send()

    @pl.when(has_after)
    def _():
        for s in range(slots):
            relay(s).wait_send()


def solution(mesh):
    planes, lines = mesh.shape["sweep"], mesh.shape["span"]

    def local(inverses, couplings, rhs, previous, slot_layer):
        slots, size, width = previous.shape[2:]
        inverses = inverses.reshape(slots, size, size)
        couplings = couplings.reshape(6, slots, size, size)
        flat = (slots, size, width)
        hbm = pl.BlockSpec(memory_space=pl.ANY)
        vmem = pl.BlockSpec(memory_space=pltpu.VMEM)
        smem = pl.BlockSpec(memory_space=pltpu.SMEM)
        thin = pltpu.VMEM(flat, jnp.bfloat16)
        wide = pltpu.VMEM(flat, jnp.float32)
        square = pltpu.VMEM((slots, size, size), jnp.bfloat16)
        result = pl.pallas_call(
            functools.partial(kernel, planes, lines),
            out_shape=jax.ShapeDtypeStruct(flat, jnp.float32),
            in_specs=[smem, hbm, hbm, hbm, hbm],
            out_specs=vmem,
            scratch_shapes=[
                square,
                pltpu.VMEM((6, slots, size, size), jnp.bfloat16),
                thin, thin, thin, thin, thin,
                wide,
                square, square,
                wide,
                pltpu.SemaphoreType.DMA((9,)),
                pltpu.SemaphoreType.DMA((3, slots)),
                pltpu.SemaphoreType.DMA((3, slots)),
                pltpu.SemaphoreType.DMA((slots,)),
                pltpu.SemaphoreType.DMA((slots,)),
            ],
            compiler_params=pltpu.CompilerParams(
                collective_id=0,
                has_side_effects=True,
                vmem_limit_bytes=60 * 1024 * 1024,
            ),
            cost_estimate=pl.CostEstimate(
                flops=18 * slots * size * size * width,
                bytes_accessed=16 * slots * size * size,
                transcendentals=0,
            ),
        )(slot_layer.reshape(slots), inverses, couplings,
          rhs.reshape(flat), previous.reshape(flat))
        return result.reshape(1, 1, *flat)

    return jax.shard_map(
        local,
        mesh=mesh,
        in_specs=(
            P("sweep", "span", None, None, None),
            P(None, "sweep", "span", None, None, None),
            P("sweep", "span", None, None, None),
            P("sweep", "span", None, None, None),
            P("sweep", "span", None),
        ),
        out_specs=P("sweep", "span", None, None, None),
        check_vma=False,
    )
```

```python
import functools

import jax
import jax.numpy as jnp
from jax import lax
from jax.experimental import pallas as pl
from jax.experimental.pallas import tpu as pltpu
from jax.sharding import PartitionSpec as P

MESH = pl.DeviceIdType.MESH


def split(value):
    high = value.astype(jnp.bfloat16)
    low = (value - high.astype(jnp.float32)).astype(jnp.bfloat16)
    return high, low


def mul(a, b):
    return jnp.dot(a, b, preferred_element_type=jnp.float32)


def kernel(
    planes, lines,
    layer, inv_hbm, coup_hbm, rhs_hbm, prev_hbm,
    out,
    inv, coup, rhs, prev, lower, upper, down,
    high, low, mate_high, mate_low, both_high, both_low,
    part, offset, mate, inflow, fresh,
    load_sem, halo_send, halo_recv, map_send, map_recv,
    mate_send, mate_recv, pass_send, relay_send, relay_recv,
):
    slots, size, width = prev.shape
    me = lax.axis_index("sweep")
    line = lax.axis_index("span")
    odd = lax.rem(me, 2) == 1
    even = jnp.logical_not(odd)
    first = me < 2
    later = jnp.logical_not(first)
    has_up = me > 0
    has_after = me < planes - 1
    takes = jnp.logical_and(odd, later)
    gives = jnp.logical_and(odd, me < planes - 2)
    left = {"span": lax.rem(line + lines - 1, lines)}
    right = {"span": lax.rem(line + 1, lines)}
    up = {"sweep": jnp.maximum(me - 1, 0)}
    after = {"sweep": jnp.minimum(me + 1, planes - 1)}
    behind = {"sweep": jnp.maximum(me - 2, 0)}
    ahead = {"sweep": jnp.minimum(me + 2, planes - 1)}

    pairs = [(prev_hbm, prev), (inv_hbm, inv), (rhs_hbm, rhs)]
    loads = [
        pltpu.make_async_copy(a, b, load_sem.at[k]) for k, (a, b) in enumerate(pairs)
    ]
    faces = [
        pltpu.make_async_copy(coup_hbm.at[f], coup.at[f], load_sem.at[len(pairs) + f])
        for f in range(6)
    ]
    for copy in (loads[1], faces[0], loads[0], faces[4], faces[5], loads[2]):
        copy.start()
    for copy in faces[1:4]:
        copy.start()

    barrier = pltpu.get_barrier_semaphore()

    def greet(device):
        pl.semaphore_signal(barrier, inc=1, device_id=device, device_id_type=MESH)

    greet(left)
    greet(right)
    expected = jnp.int32(2)
    for there, device in ((has_up, up), (has_after, after), (takes, behind), (gives, ahead)):
        pl.when(there)(functools.partial(greet, device))
        expected = expected + there.astype(jnp.int32)
    pl.semaphore_wait(barrier, expected)

    def send(src, dst, send_sem, recv_sem, device):
        return pltpu.make_async_remote_copy(
            src_ref=src,
            dst_ref=dst,
            send_sem=send_sem,
            recv_sem=recv_sem,
            device_id=device,
            device_id_type=MESH,
        )

    def halo(kind, s):
        target, ref = ((right, lower), (left, upper), (up, down))[kind]
        return send(prev_hbm.at[s], ref.at[s], halo_send.at[kind, s], halo_recv.at[kind, s], target)

    def give_map(k):
        src, dst = ((high, mate_high), (low, mate_low))[k]
        return send(src, dst, map_send.at[k], map_recv.at[k], after)

    def give_offset(s):
        return send(offset.at[s], mate.at[s], mate_send.at[s], mate_recv.at[s], after)

    def pass_on(s):
        return send(inflow.at[s], inflow.at[s], pass_send.at[s], relay_recv.at[s], up)

    def relay(s):
        return send(fresh.at[s], inflow.at[s], relay_send.at[s], relay_recv.at[s], ahead)

    for s in range(slots):
        halo(0, s).start()
        halo(1, s).start()

    @pl.when(has_up)
    def _():
        for s in range(slots):
            halo(2, s).start()

    @pl.when(jnp.logical_not(has_after))
    def _():
        down[...] = jnp.zeros_like(down)

    loads[1].wait()
    faces[0].wait()
    for s in range(slots):
        high[s], low[s] = split(-mul(inv[s], coup[0, s]))

    @pl.when(jnp.logical_and(even, later))
    def _():
        give_map(0).start()
        give_map(1).start()

    loads[0].wait()
    faces[4].wait()
    faces[5].wait()
    loads[2].wait()

    for s in range(slots):
        total = rhs[s].astype(jnp.float32)
        for face, step in ((4, -1), (5, 1)):
            wanted = layer[s] + step
            found = jnp.int32(0)
            known = jnp.int32(0)
            for t in range(slots):
                hit = (layer[t] == wanted).astype(jnp.int32)
                found = found + t * hit
                known = known + hit
            vector = prev[found].astype(jnp.float32) * known.astype(jnp.float32)
            total = total - mul(coup[face, s], vector.astype(jnp.bfloat16))
        part[s] = total

    for copy in faces[1:4]:
        copy.wait()

    @pl.when(takes)
    def _():
        give_map(0).wait_recv()
        give_map(1).wait_recv()
        for s in range(slots):
            one, two = mate_high[s], mate_low[s]
            product = mul(high[s], one) + (mul(high[s], two) + mul(low[s], one))
            both_high[s], both_low[s] = split(product)

    def apply_map(matrix_high, matrix_low, vector):
        one, two = split(vector)
        wide = mul(matrix_high, jnp.concatenate([one, two], axis=1))
        return wide[:, :width] + (wide[:, width:] + mul(matrix_low, one))

    def put(s, value):
        out[s, :, 0, :] = value

    for k in range(slots + 1):
        if k < slots:
            s = k
            halo(0, s).wait_recv()
            halo(1, s).wait_recv()
            pl.when(has_after)(halo(2, s).wait_recv)
            coupled = mul(coup[1, s], down[s])
            coupled = coupled + mul(coup[2, s], lower[s])
            coupled = coupled + mul(coup[3, s], upper[s])
            forcing = (part[s] - coupled).astype(jnp.bfloat16)
            offset[s] = mul(inv[s], forcing)
            pl.when(even)(give_offset(s).start)

            @pl.when(odd)
            def _(s=s):
                give_offset(s).wait_recv()
                fresh[s] = offset[s] + apply_map(high[s], low[s], mate[s])

            @pl.when(jnp.logical_and(odd, first))
            def _(s=s):
                pl.when(gives)(relay(s).start)
                put(s, fresh[s])

        if k > 0:
            s = k - 1

            @pl.when(takes)
            def _(s=s):
                relay(s).wait_recv()
                pass_on(s).start()
                fresh[s] = fresh[s] + apply_map(both_high[s], both_low[s], inflow[s])
                pl.when(gives)(relay(s).start)
                put(s, fresh[s])

    @pl.when(even)
    def _():
        @pl.when(first)
        def _():
            for s in range(slots):
                put(s, offset[s])

        @pl.when(later)
        def _():
            for s in range(slots):
                relay(s).wait_recv()
                put(s, offset[s] + apply_map(high[s], low[s], inflow[s]))
            give_map(0).wait_send()
            give_map(1).wait_send()

        for s in range(slots):
            give_offset(s).wait_send()

    for s in range(slots):
        halo(0, s).wait_send()
        halo(1, s).wait_send()

    @pl.when(has_up)
    def _():
        for s in range(slots):
            halo(2, s).wait_send()

    @pl.when(takes)
    def _():
        for s in range(slots):
            pass_on(s).wait_send()

    @pl.when(gives)
    def _():
        for s in range(slots):
            relay(s).wait_send()


def solution(mesh):
    planes, lines = mesh.shape["sweep"], mesh.shape["span"]

    def local(inverses, couplings, rhs, previous, slot_layer):
        slots, size, width = previous.shape[2:]
        inverses = inverses.reshape(slots, size, size)
        couplings = couplings.reshape(6, slots, size, size)
        flat = (slots, size, width)
        hbm = pl.BlockSpec(memory_space=pl.ANY)
        vmem = pl.BlockSpec(memory_space=pltpu.VMEM)
        smem = pl.BlockSpec(memory_space=pltpu.SMEM)
        thin = pltpu.VMEM(flat, jnp.bfloat16)
        wide = pltpu.VMEM(flat, jnp.float32)
        square = pltpu.VMEM((slots, size, size), jnp.bfloat16)
        dma = pltpu.SemaphoreType.DMA
        result = pl.pallas_call(
            functools.partial(kernel, planes, lines),
            out_shape=jax.ShapeDtypeStruct((slots, size, 1, width), jnp.float32),
            in_specs=[smem, hbm, hbm, hbm, hbm],
            out_specs=vmem,
            scratch_shapes=[
                square,
                pltpu.VMEM((6, slots, size, size), jnp.bfloat16),
                thin, thin, thin, thin, thin,
                square, square, square, square, square, square,
                wide, wide, wide, wide, wide,
                dma((9,)),
                dma((3, slots)),
                dma((3, slots)),
                dma((2,)),
                dma((2,)),
                dma((slots,)),
                dma((slots,)),
                dma((slots,)),
                dma((slots,)),
                dma((slots,)),
            ],
            compiler_params=pltpu.CompilerParams(
                collective_id=0,
                has_side_effects=True,
                vmem_limit_bytes=60 * 1024 * 1024,
            ),
            cost_estimate=pl.CostEstimate(
                flops=18 * slots * size * size * width,
                bytes_accessed=16 * slots * size * size,
                transcendentals=0,
            ),
        )(slot_layer.reshape(slots), inverses, couplings,
          rhs.reshape(flat), previous.reshape(flat))
        return result.reshape(1, 1, *flat)

    return jax.shard_map(
        local,
        mesh=mesh,
        in_specs=(
            P("sweep", "span", None, None, None),
            P(None, "sweep", "span", None, None, None),
            P("sweep", "span", None, None, None),
            P("sweep", "span", None, None, None),
            P("sweep", "span", None),
        ),
        out_specs=P("sweep", "span", None, None, None),
        check_vma=False,
    )
```

```python
import functools

import jax
import jax.numpy as jnp
from jax import lax
from jax.experimental import pallas as pl
from jax.experimental.pallas import tpu as pltpu
from jax.sharding import PartitionSpec as P

MESH = pl.DeviceIdType.MESH


def split(value):
    high = value.astype(jnp.bfloat16)
    low = (value - high.astype(jnp.float32)).astype(jnp.bfloat16)
    return high, low


def mul(a, b):
    return jnp.dot(a, b, preferred_element_type=jnp.float32)


def kernel(
    planes, lines,
    layer, inv_hbm, coup_hbm, rhs_hbm, prev_hbm,
    out,
    inv, coup, rhs, prev, lower, upper, down,
    high, low, mate_high, mate_low, both_high, both_low,
    part, offset, mate, fresh, halves, inflow,
    load_sem, halo_send, halo_recv, map_send, map_recv,
    mate_send, mate_recv, pass_send, relay_send, relay_recv,
):
    slots, size, width = prev.shape
    me = lax.axis_index("sweep")
    line = lax.axis_index("span")
    odd = lax.rem(me, 2) == 1
    even = jnp.logical_not(odd)
    first = me < 2
    later = jnp.logical_not(first)
    has_up = me > 0
    has_after = me < planes - 1
    takes = jnp.logical_and(odd, later)
    gives = jnp.logical_and(odd, me < planes - 2)
    left = {"span": lax.rem(line + lines - 1, lines)}
    right = {"span": lax.rem(line + 1, lines)}
    up = {"sweep": jnp.maximum(me - 1, 0)}
    after = {"sweep": jnp.minimum(me + 1, planes - 1)}
    behind = {"sweep": jnp.maximum(me - 2, 0)}
    ahead = {"sweep": jnp.minimum(me + 2, planes - 1)}

    pairs = [(prev_hbm, prev), (inv_hbm, inv), (rhs_hbm, rhs)]
    loads = [
        pltpu.make_async_copy(a, b, load_sem.at[k]) for k, (a, b) in enumerate(pairs)
    ]
    faces = [
        pltpu.make_async_copy(coup_hbm.at[f], coup.at[f], load_sem.at[len(pairs) + f])
        for f in range(6)
    ]
    for copy in (loads[1], faces[0], loads[0], faces[4], faces[5], loads[2]):
        copy.start()
    for copy in faces[1:4]:
        copy.start()

    barrier = pltpu.get_barrier_semaphore()

    def greet(device):
        pl.semaphore_signal(barrier, inc=1, device_id=device, device_id_type=MESH)

    greet(left)
    greet(right)
    expected = jnp.int32(2)
    for there, device in ((has_up, up), (has_after, after), (takes, behind), (gives, ahead)):
        pl.when(there)(functools.partial(greet, device))
        expected = expected + there.astype(jnp.int32)
    pl.semaphore_wait(barrier, expected)

    def send(src, dst, send_sem, recv_sem, device):
        return pltpu.make_async_remote_copy(
            src_ref=src,
            dst_ref=dst,
            send_sem=send_sem,
            recv_sem=recv_sem,
            device_id=device,
            device_id_type=MESH,
        )

    def halo(kind, s):
        target, ref = ((right, lower), (left, upper), (up, down))[kind]
        return send(prev_hbm.at[s], ref.at[s], halo_send.at[kind, s], halo_recv.at[kind, s], target)

    def give_map(k):
        src, dst = ((high, mate_high), (low, mate_low))[k]
        return send(src, dst, map_send.at[k], map_recv.at[k], after)

    def give_offset(s):
        return send(offset.at[s], mate.at[s], mate_send.at[s], mate_recv.at[s], after)

    def pass_on(p, s):
        place = inflow.at[p, s]
        return send(place, place, pass_send.at[p, s], relay_recv.at[p, s], up)

    def relay(p, s):
        src, dst = halves.at[p, s], inflow.at[p, s]
        return send(src, dst, relay_send.at[p, s], relay_recv.at[p, s], ahead)

    for s in range(slots):
        halo(0, s).start()
        halo(1, s).start()

    @pl.when(has_up)
    def _():
        for s in range(slots):
            halo(2, s).start()

    @pl.when(jnp.logical_not(has_after))
    def _():
        down[...] = jnp.zeros_like(down)

    loads[1].wait()
    faces[0].wait()
    for s in range(slots):
        high[s], low[s] = split(-mul(inv[s], coup[0, s]))

    @pl.when(jnp.logical_and(even, later))
    def _():
        give_map(0).start()
        give_map(1).start()

    loads[0].wait()
    faces[4].wait()
    faces[5].wait()
    loads[2].wait()

    for s in range(slots):
        total = rhs[s].astype(jnp.float32)
        for face, step in ((4, -1), (5, 1)):
            wanted = layer[s] + step
            found = jnp.int32(0)
            known = jnp.int32(0)
            for t in range(slots):
                hit = (layer[t] == wanted).astype(jnp.int32)
                found = found + t * hit
                known = known + hit
            vector = prev[found].astype(jnp.float32) * known.astype(jnp.float32)
            total = total - mul(coup[face, s], vector.astype(jnp.bfloat16))
        part[s] = total

    for copy in faces[1:4]:
        copy.wait()

    @pl.when(takes)
    def _():
        give_map(0).wait_recv()
        give_map(1).wait_recv()
        for s in range(slots):
            one, two = mate_high[s], mate_low[s]
            product = mul(high[s], one) + (mul(high[s], two) + mul(low[s], one))
            both_high[s], both_low[s] = split(product)

    def apply_map(matrix_high, matrix_low, vector):
        one, two = split(vector)
        wide = mul(matrix_high, jnp.concatenate([one, two], axis=1))
        return wide[:, :width] + (wide[:, width:] + mul(matrix_low, one))

    def put(s, value):
        out[s, :, 0, :] = value

    def emit(s, value):
        halves[0, s], halves[1, s] = split(value)

        @pl.when(gives)
        def _():
            relay(0, s).start()
            relay(1, s).start()

        put(s, value)

    def arrive(s, matrix_high, matrix_low, start, forward):
        relay(0, s).wait_recv()
        if forward:
            pass_on(0, s).start()
        one = inflow[0, s]
        value = start[s] + (mul(matrix_high[s], one) + mul(matrix_low[s], one))
        relay(1, s).wait_recv()
        if forward:
            pass_on(1, s).start()
        return value + mul(matrix_high[s], inflow[1, s])

    for k in range(slots + 1):
        if k < slots:
            s = k
            halo(0, s).wait_recv()
            halo(1, s).wait_recv()
            pl.when(has_after)(halo(2, s).wait_recv)
            coupled = mul(coup[1, s], down[s])
            coupled = coupled + mul(coup[2, s], lower[s])
            coupled = coupled + mul(coup[3, s], upper[s])
            forcing = (part[s] - coupled).astype(jnp.bfloat16)
            offset[s] = mul(inv[s], forcing)
            pl.when(even)(give_offset(s).start)

            @pl.when(odd)
            def _(s=s):
                give_offset(s).wait_recv()
                fresh[s] = offset[s] + apply_map(high[s], low[s], mate[s])

            @pl.when(jnp.logical_and(odd, first))
            def _(s=s):
                emit(s, fresh[s])

        if k > 0:
            s = k - 1

            @pl.when(takes)
            def _(s=s):
                emit(s, arrive(s, both_high, both_low, fresh, True))

    @pl.when(even)
    def _():
        @pl.when(first)
        def _():
            for s in range(slots):
                put(s, offset[s])

        @pl.when(later)
        def _():
            for s in range(slots):
                put(s, arrive(s, high, low, offset, False))
            give_map(0).wait_send()
            give_map(1).wait_send()

        for s in range(slots):
            give_offset(s).wait_send()

    for s in range(slots):
        halo(0, s).wait_send()
        halo(1, s).wait_send()

    @pl.when(has_up)
    def _():
        for s in range(slots):
            halo(2, s).wait_send()

    @pl.when(takes)
    def _():
        for s in range(slots):
            pass_on(0, s).wait_send()
            pass_on(1, s).wait_send()

    @pl.when(gives)
    def _():
        for s in range(slots):
            relay(0, s).wait_send()
            relay(1, s).wait_send()


def copy_kernel(src, dst, sem):
    copies = [
        pltpu.make_async_copy(src.at[s], dst.at[s], sem.at[s]) for s in range(src.shape[0])
    ]
    for copy in copies:
        copy.start()
    for copy in copies:
        copy.wait()


def solution(mesh):
    planes, lines = mesh.shape["sweep"], mesh.shape["span"]

    def local(inverses, couplings, rhs, previous, slot_layer):
        slots, size, width = previous.shape[2:]
        inverses = inverses.reshape(slots, size, size)
        couplings = couplings.reshape(6, slots, size, size)
        flat = (slots, size, width)
        hbm = pl.BlockSpec(memory_space=pl.ANY)
        vmem = pl.BlockSpec(memory_space=pltpu.VMEM)
        smem = pl.BlockSpec(memory_space=pltpu.SMEM)
        thin = pltpu.VMEM(flat, jnp.bfloat16)
        wide = pltpu.VMEM(flat, jnp.float32)
        square = pltpu.VMEM((slots, size, size), jnp.bfloat16)
        dma = pltpu.SemaphoreType.DMA
        result = pl.pallas_call(
            functools.partial(kernel, planes, lines),
            out_shape=jax.ShapeDtypeStruct((slots, size, 1, width), jnp.float32),
            in_specs=[smem, hbm, hbm, hbm, hbm],
            out_specs=vmem,
            scratch_shapes=[
                square,
                pltpu.VMEM((6, slots, size, size), jnp.bfloat16),
                thin, thin, thin, thin, thin,
                square, square, square, square, square, square,
                wide, wide, wide, wide,
                pltpu.VMEM((2, *flat), jnp.bfloat16),
                pltpu.VMEM((2, *flat), jnp.bfloat16),
                dma((9,)),
                dma((3, slots)),
                dma((3, slots)),
                dma((2,)),
                dma((2,)),
                dma((slots,)),
                dma((slots,)),
                dma((2, slots)),
                dma((2, slots)),
                dma((2, slots)),
            ],
            compiler_params=pltpu.CompilerParams(
                collective_id=0,
                has_side_effects=True,
                vmem_limit_bytes=60 * 1024 * 1024,
            ),
            cost_estimate=pl.CostEstimate(
                flops=18 * slots * size * size * width,
                bytes_accessed=16 * slots * size * size,
                transcendentals=0,
            ),
        )(slot_layer.reshape(slots), inverses, couplings,
          rhs.reshape(flat), previous.reshape(flat))
        result = pl.pallas_call(
            copy_kernel,
            out_shape=jax.ShapeDtypeStruct(result.shape, result.dtype),
            in_specs=[hbm],
            out_specs=hbm,
            scratch_shapes=[dma((slots,))],
        )(result)
        return result.reshape(1, 1, *flat)

    return jax.shard_map(
        local,
        mesh=mesh,
        in_specs=(
            P("sweep", "span", None, None, None),
            P(None, "sweep", "span", None, None, None),
            P("sweep", "span", None, None, None),
            P("sweep", "span", None, None, None),
            P("sweep", "span", None),
        ),
        out_specs=P("sweep", "span", None, None, None),
        check_vma=False,
    )
```

```python
import functools

import jax
import jax.numpy as jnp
from jax import lax
from jax.experimental import pallas as pl
from jax.experimental.pallas import tpu as pltpu
from jax.sharding import PartitionSpec as P

MESH = pl.DeviceIdType.MESH


def split(value):
    high = value.astype(jnp.bfloat16)
    low = (value - high.astype(jnp.float32)).astype(jnp.bfloat16)
    return high, low


def mul(a, b):
    return jnp.dot(a, b, preferred_element_type=jnp.float32)


def kernel(
    planes, lines,
    layer, inv_hbm, coup_hbm, rhs_hbm, prev_hbm,
    out,
    inv, coup, rhs, prev, lower, upper, down,
    high, low, mate_high, mate_low, both_high, both_low,
    part, offset, mate, inflow, fresh, rows,
    load_sem, store_sem, halo_send, halo_recv, map_send, map_recv,
    mate_send, mate_recv, pass_send, relay_send, relay_recv,
):
    slots, size, width = prev.shape
    me = lax.axis_index("sweep")
    line = lax.axis_index("span")
    odd = lax.rem(me, 2) == 1
    even = jnp.logical_not(odd)
    first = me < 2
    later = jnp.logical_not(first)
    has_up = me > 0
    has_after = me < planes - 1
    takes = jnp.logical_and(odd, later)
    gives = jnp.logical_and(odd, me < planes - 2)
    left = {"span": lax.rem(line + lines - 1, lines)}
    right = {"span": lax.rem(line + 1, lines)}
    up = {"sweep": jnp.maximum(me - 1, 0)}
    after = {"sweep": jnp.minimum(me + 1, planes - 1)}
    behind = {"sweep": jnp.maximum(me - 2, 0)}
    ahead = {"sweep": jnp.minimum(me + 2, planes - 1)}

    pairs = [(prev_hbm, prev), (inv_hbm, inv), (rhs_hbm, rhs)]
    loads = [
        pltpu.make_async_copy(a, b, load_sem.at[k]) for k, (a, b) in enumerate(pairs)
    ]
    faces = [
        pltpu.make_async_copy(coup_hbm.at[f], coup.at[f], load_sem.at[len(pairs) + f])
        for f in range(6)
    ]
    for copy in (loads[1], faces[0], loads[0], faces[4], faces[5], loads[2]):
        copy.start()
    for copy in faces[1:4]:
        copy.start()

    barrier = pltpu.get_barrier_semaphore()

    def greet(device):
        pl.semaphore_signal(barrier, inc=1, device_id=device, device_id_type=MESH)

    greet(left)
    greet(right)
    expected = jnp.int32(2)
    for there, device in ((has_up, up), (has_after, after), (takes, behind), (gives, ahead)):
        pl.when(there)(functools.partial(greet, device))
        expected = expected + there.astype(jnp.int32)
    pl.semaphore_wait(barrier, expected)

    def send(src, dst, send_sem, recv_sem, device):
        return pltpu.make_async_remote_copy(
            src_ref=src,
            dst_ref=dst,
            send_sem=send_sem,
            recv_sem=recv_sem,
            device_id=device,
            device_id_type=MESH,
        )

    def halo(kind, s):
        target, ref = ((right, lower), (left, upper), (up, down))[kind]
        return send(prev_hbm.at[s], ref.at[s], halo_send.at[kind, s], halo_recv.at[kind, s], target)

    def give_map(k):
        src, dst = ((high, mate_high), (low, mate_low))[k]
        return send(src, dst, map_send.at[k], map_recv.at[k], after)

    def give_offset(s):
        return send(offset.at[s], mate.at[s], mate_send.at[s], mate_recv.at[s], after)

    def pass_on(s):
        return send(inflow.at[s], inflow.at[s], pass_send.at[s], relay_recv.at[s], up)

    def relay(s):
        return send(fresh.at[s], inflow.at[s], relay_send.at[s], relay_recv.at[s], ahead)

    for s in range(slots):
        halo(0, s).start()
        halo(1, s).start()

    @pl.when(has_up)
    def _():
        for s in range(slots):
            halo(2, s).start()

    @pl.when(jnp.logical_not(has_after))
    def _():
        down[...] = jnp.zeros_like(down)

    loads[1].wait()
    faces[0].wait()
    for s in range(slots):
        high[s], low[s] = split(-mul(inv[s], coup[0, s]))

    @pl.when(jnp.logical_and(even, later))
    def _():
        give_map(0).start()
        give_map(1).start()

    loads[0].wait()
    faces[4].wait()
    faces[5].wait()
    loads[2].wait()

    for s in range(slots):
        total = rhs[s].astype(jnp.float32)
        for face, step in ((4, -1), (5, 1)):
            wanted = layer[s] + step
            found = jnp.int32(0)
            known = jnp.int32(0)
            for t in range(slots):
                hit = (layer[t] == wanted).astype(jnp.int32)
                found = found + t * hit
                known = known + hit
            vector = prev[found].astype(jnp.float32) * known.astype(jnp.float32)
            total = total - mul(coup[face, s], vector.astype(jnp.bfloat16))
        part[s] = total

    for copy in faces[1:4]:
        copy.wait()

    @pl.when(takes)
    def _():
        give_map(0).wait_recv()
        give_map(1).wait_recv()
        for s in range(slots):
            one, two = mate_high[s], mate_low[s]
            product = mul(high[s], one) + (mul(high[s], two) + mul(low[s], one))
            both_high[s], both_low[s] = split(product)

    def apply_map(matrix_high, matrix_low, vector):
        one, two = split(vector)
        wide = mul(matrix_high, jnp.concatenate([one, two], axis=1))
        return wide[:, :width] + (wide[:, width:] + mul(matrix_low, one))

    def store(s):
        return pltpu.make_async_copy(rows.at[s], out.at[s], store_sem.at[s])

    def put(s, value):
        rows[s, :, 0, :] = value
        store(s).start()

    for k in range(slots + 1):
        if k < slots:
            s = k
            halo(0, s).wait_recv()
            halo(1, s).wait_recv()
            pl.when(has_after)(halo(2, s).wait_recv)
            coupled = mul(coup[1, s], down[s])
            coupled = coupled + mul(coup[2, s], lower[s])
            coupled = coupled + mul(coup[3, s], upper[s])
            forcing = (part[s] - coupled).astype(jnp.bfloat16)
            offset[s] = mul(inv[s], forcing)
            pl.when(even)(give_offset(s).start)

            @pl.when(odd)
            def _(s=s):
                give_offset(s).wait_recv()
                fresh[s] = offset[s] + apply_map(high[s], low[s], mate[s])

            @pl.when(jnp.logical_and(odd, first))
            def _(s=s):
                pl.when(gives)(relay(s).start)
                put(s, fresh[s])

        if k > 0:
            s = k - 1

            @pl.when(takes)
            def _(s=s):
                relay(s).wait_recv()
                pass_on(s).start()
                fresh[s] = fresh[s] + apply_map(both_high[s], both_low[s], inflow[s])
                pl.when(gives)(relay(s).start)
                put(s, fresh[s])

    @pl.when(even)
    def _():
        @pl.when(first)
        def _():
            for s in range(slots):
                put(s, offset[s])

        @pl.when(later)
        def _():
            for s in range(slots):
                relay(s).wait_recv()
                put(s, offset[s] + apply_map(high[s], low[s], inflow[s]))
            give_map(0).wait_send()
            give_map(1).wait_send()

        for s in range(slots):
            give_offset(s).wait_send()

    for s in range(slots):
        store(s).wait()
        halo(0, s).wait_send()
        halo(1, s).wait_send()

    @pl.when(has_up)
    def _():
        for s in range(slots):
            halo(2, s).wait_send()

    @pl.when(takes)
    def _():
        for s in range(slots):
            pass_on(s).wait_send()

    @pl.when(gives)
    def _():
        for s in range(slots):
            relay(s).wait_send()


def move(src, dst, held, load_sem, store_sem):
    slots = src.shape[0]
    loads = [
        pltpu.make_async_copy(src.at[s], held.at[s], load_sem.at[s]) for s in range(slots)
    ]
    stores = [
        pltpu.make_async_copy(held.at[s], dst.at[s], store_sem.at[s]) for s in range(slots)
    ]
    for load in loads:
        load.start()
    for load, store in zip(loads, stores):
        load.wait()
        store.start()
    for store in stores:
        store.wait()


def solution(mesh):
    planes, lines = mesh.shape["sweep"], mesh.shape["span"]

    def local(inverses, couplings, rhs, previous, slot_layer):
        slots, size, width = previous.shape[2:]
        inverses = inverses.reshape(slots, size, size)
        couplings = couplings.reshape(6, slots, size, size)
        flat = (slots, size, width)
        hbm = pl.BlockSpec(memory_space=pl.ANY)
        smem = pl.BlockSpec(memory_space=pltpu.SMEM)
        thin = pltpu.VMEM(flat, jnp.bfloat16)
        wide = pltpu.VMEM(flat, jnp.float32)
        square = pltpu.VMEM((slots, size, size), jnp.bfloat16)
        dma = pltpu.SemaphoreType.DMA
        result = pl.pallas_call(
            functools.partial(kernel, planes, lines),
            out_shape=jax.ShapeDtypeStruct((slots, size, 1, width), jnp.float32),
            in_specs=[smem, hbm, hbm, hbm, hbm],
            out_specs=hbm,
            scratch_shapes=[
                square,
                pltpu.VMEM((6, slots, size, size), jnp.bfloat16),
                thin, thin, thin, thin, thin,
                square, square, square, square, square, square,
                wide, wide, wide, wide, wide,
                pltpu.VMEM((slots, size, 1, width), jnp.float32),
                dma((9,)),
                dma((slots,)),
                dma((3, slots)),
                dma((3, slots)),
                dma((2,)),
                dma((2,)),
                dma((slots,)),
                dma((slots,)),
                dma((slots,)),
                dma((slots,)),
                dma((slots,)),
            ],
            compiler_params=pltpu.CompilerParams(
                collective_id=0,
                has_side_effects=True,
                vmem_limit_bytes=60 * 1024 * 1024,
            ),
            cost_estimate=pl.CostEstimate(
                flops=18 * slots * size * size * width,
                bytes_accessed=16 * slots * size * size,
                transcendentals=0,
            ),
        )(slot_layer.reshape(slots), inverses, couplings,
          rhs.reshape(flat), previous.reshape(flat))
        result = pl.pallas_call(
            move,
            out_shape=jax.ShapeDtypeStruct(result.shape, result.dtype),
            in_specs=[hbm],
            out_specs=hbm,
            scratch_shapes=[
                pltpu.VMEM(result.shape, result.dtype), dma((slots,)), dma((slots,)),
            ],
            compiler_params=pltpu.CompilerParams(vmem_limit_bytes=60 * 1024 * 1024),
        )(result)
        return result.reshape(1, 1, *flat)

    return jax.shard_map(
        local,
        mesh=mesh,
        in_specs=(
            P("sweep", "span", None, None, None),
            P(None, "sweep", "span", None, None, None),
            P("sweep", "span", None, None, None),
            P("sweep", "span", None, None, None),
            P("sweep", "span", None),
        ),
        out_specs=P("sweep", "span", None, None, None),
        check_vma=False,
    )
```

```python
import functools

import jax
import jax.numpy as jnp
from jax import lax
from jax.experimental import pallas as pl
from jax.experimental.pallas import tpu as pltpu
from jax.sharding import PartitionSpec as P

MESH = pl.DeviceIdType.MESH


def split(value):
    high = value.astype(jnp.bfloat16)
    low = (value - high.astype(jnp.float32)).astype(jnp.bfloat16)
    return high, low


def mul(a, b):
    return jnp.dot(a, b, preferred_element_type=jnp.float32)


def kernel(
    planes, lines,
    layer, inv_hbm, coup_hbm, rhs_hbm, prev_hbm,
    out,
    inv, coup, rhs, prev, lower, upper, down,
    high, low, mate_high, mate_low, both_high, both_low,
    part, offset, mate, inflow, fresh, rows,
    load_sem, store_sem, halo_send, halo_recv, map_send, map_recv,
    mate_send, mate_recv, pass_send, relay_send, relay_recv,
):
    slots, size, width = prev.shape
    me = lax.axis_index("sweep")
    line = lax.axis_index("span")
    odd = lax.rem(me, 2) == 1
    even = jnp.logical_not(odd)
    first = me < 2
    later = jnp.logical_not(first)
    has_up = me > 0
    has_after = me < planes - 1
    takes = jnp.logical_and(odd, later)
    gives = jnp.logical_and(odd, me < planes - 2)
    left = {"span": lax.rem(line + lines - 1, lines)}
    right = {"span": lax.rem(line + 1, lines)}
    up = {"sweep": jnp.maximum(me - 1, 0)}
    after = {"sweep": jnp.minimum(me + 1, planes - 1)}
    behind = {"sweep": jnp.maximum(me - 2, 0)}
    ahead = {"sweep": jnp.minimum(me + 2, planes - 1)}

    pairs = [(prev_hbm, prev), (inv_hbm, inv), (rhs_hbm, rhs)]
    loads = [
        pltpu.make_async_copy(a, b, load_sem.at[k]) for k, (a, b) in enumerate(pairs)
    ]
    faces = [
        pltpu.make_async_copy(coup_hbm.at[f], coup.at[f], load_sem.at[len(pairs) + f])
        for f in range(6)
    ]
    for copy in (loads[1], faces[0], loads[0], faces[4], faces[5], loads[2]):
        copy.start()
    for copy in faces[1:4]:
        copy.start()

    barrier = pltpu.get_barrier_semaphore()

    def greet(device):
        pl.semaphore_signal(barrier, inc=1, device_id=device, device_id_type=MESH)

    greet(left)
    greet(right)
    expected = jnp.int32(2)
    for there, device in ((has_up, up), (has_after, after), (takes, behind), (gives, ahead)):
        pl.when(there)(functools.partial(greet, device))
        expected = expected + there.astype(jnp.int32)
    pl.semaphore_wait(barrier, expected)

    def send(src, dst, send_sem, recv_sem, device):
        return pltpu.make_async_remote_copy(
            src_ref=src,
            dst_ref=dst,
            send_sem=send_sem,
            recv_sem=recv_sem,
            device_id=device,
            device_id_type=MESH,
        )

    def halo(kind, s):
        target, ref = ((right, lower), (left, upper), (up, down))[kind]
        return send(prev_hbm.at[s], ref.at[s], halo_send.at[kind, s], halo_recv.at[kind, s], target)

    def give_map(k):
        src, dst = ((high, mate_high), (low, mate_low))[k]
        return send(src, dst, map_send.at[k], map_recv.at[k], after)

    def give_offset(s):
        return send(offset.at[s], mate.at[s], mate_send.at[s], mate_recv.at[s], after)

    def pass_on(s):
        return send(inflow.at[s], inflow.at[s], pass_send.at[s], relay_recv.at[s], up)

    def relay(s):
        return send(fresh.at[s], inflow.at[s], relay_send.at[s], relay_recv.at[s], ahead)

    def send_halo():
        for s in range(slots):
            halo(0, s).start()
            halo(1, s).start()

    pl.when(even)(send_halo)

    @pl.when(has_up)
    def _():
        for s in range(slots):
            halo(2, s).start()

    @pl.when(jnp.logical_not(has_after))
    def _():
        down[...] = jnp.zeros_like(down)

    loads[1].wait()
    faces[0].wait()
    for s in range(slots):
        high[s], low[s] = split(-mul(inv[s], coup[0, s]))

    pl.when(odd)(send_halo)

    @pl.when(jnp.logical_and(even, later))
    def _():
        give_map(0).start()
        give_map(1).start()

    loads[0].wait()
    faces[4].wait()
    faces[5].wait()
    loads[2].wait()

    for s in range(slots):
        total = rhs[s].astype(jnp.float32)
        for face, step in ((4, -1), (5, 1)):
            wanted = layer[s] + step
            found = jnp.int32(0)
            known = jnp.int32(0)
            for t in range(slots):
                hit = (layer[t] == wanted).astype(jnp.int32)
                found = found + t * hit
                known = known + hit
            vector = prev[found].astype(jnp.float32) * known.astype(jnp.float32)
            total = total - mul(coup[face, s], vector.astype(jnp.bfloat16))
        part[s] = total

    for copy in faces[1:4]:
        copy.wait()

    @pl.when(takes)
    def _():
        give_map(0).wait_recv()
        give_map(1).wait_recv()
        for s in range(slots):
            one, two = mate_high[s], mate_low[s]
            product = mul(high[s], one) + (mul(high[s], two) + mul(low[s], one))
            both_high[s], both_low[s] = split(product)

    def apply_map(matrix_high, matrix_low, vector):
        one, two = split(vector)
        wide = mul(matrix_high, jnp.concatenate([one, two], axis=1))
        return wide[:, :width] + (wide[:, width:] + mul(matrix_low, one))

    def store(s):
        return pltpu.make_async_copy(rows.at[s], out.at[s], store_sem.at[s])

    def put(s, value):
        rows[s, :, 0, :] = value
        store(s).start()

    for k in range(slots + 1):
        if k < slots:
            s = k
            halo(0, s).wait_recv()
            halo(1, s).wait_recv()
            pl.when(has_after)(halo(2, s).wait_recv)
            coupled = mul(coup[1, s], down[s])
            coupled = coupled + mul(coup[2, s], lower[s])
            coupled = coupled + mul(coup[3, s], upper[s])
            forcing = (part[s] - coupled).astype(jnp.bfloat16)
            offset[s] = mul(inv[s], forcing)
            pl.when(even)(give_offset(s).start)

            @pl.when(odd)
            def _(s=s):
                give_offset(s).wait_recv()
                fresh[s] = offset[s] + apply_map(high[s], low[s], mate[s])

            @pl.when(jnp.logical_and(odd, first))
            def _(s=s):
                pl.when(gives)(relay(s).start)
                put(s, fresh[s])

        if k > 0:
            s = k - 1

            @pl.when(takes)
            def _(s=s):
                relay(s).wait_recv()
                pass_on(s).start()
                fresh[s] = fresh[s] + apply_map(both_high[s], both_low[s], inflow[s])
                pl.when(gives)(relay(s).start)
                put(s, fresh[s])

    @pl.when(even)
    def _():
        @pl.when(first)
        def _():
            for s in range(slots):
                put(s, offset[s])

        @pl.when(later)
        def _():
            for s in range(slots):
                relay(s).wait_recv()
                put(s, offset[s] + apply_map(high[s], low[s], inflow[s]))
            give_map(0).wait_send()
            give_map(1).wait_send()

        for s in range(slots):
            give_offset(s).wait_send()

    for s in range(slots):
        store(s).wait()
        halo(0, s).wait_send()
        halo(1, s).wait_send()

    @pl.when(has_up)
    def _():
        for s in range(slots):
            halo(2, s).wait_send()

    @pl.when(takes)
    def _():
        for s in range(slots):
            pass_on(s).wait_send()

    @pl.when(gives)
    def _():
        for s in range(slots):
            relay(s).wait_send()


def move(src, dst, held, load_sem, store_sem):
    slots = src.shape[0]
    loads = [
        pltpu.make_async_copy(src.at[s], held.at[s], load_sem.at[s]) for s in range(slots)
    ]
    stores = [
        pltpu.make_async_copy(held.at[s], dst.at[s], store_sem.at[s]) for s in range(slots)
    ]
    for load in loads:
        load.start()
    for load, store in zip(loads, stores):
        load.wait()
        store.start()
    for store in stores:
        store.wait()


def solution(mesh):
    planes, lines = mesh.shape["sweep"], mesh.shape["span"]

    def local(inverses, couplings, rhs, previous, slot_layer):
        slots, size, width = previous.shape[2:]
        inverses = inverses.reshape(slots, size, size)
        couplings = couplings.reshape(6, slots, size, size)
        flat = (slots, size, width)
        hbm = pl.BlockSpec(memory_space=pl.ANY)
        smem = pl.BlockSpec(memory_space=pltpu.SMEM)
        thin = pltpu.VMEM(flat, jnp.bfloat16)
        wide = pltpu.VMEM(flat, jnp.float32)
        square = pltpu.VMEM((slots, size, size), jnp.bfloat16)
        dma = pltpu.SemaphoreType.DMA
        result = pl.pallas_call(
            functools.partial(kernel, planes, lines),
            out_shape=jax.ShapeDtypeStruct((slots, size, 1, width), jnp.float32),
            in_specs=[smem, hbm, hbm, hbm, hbm],
            out_specs=hbm,
            scratch_shapes=[
                square,
                pltpu.VMEM((6, slots, size, size), jnp.bfloat16),
                thin, thin, thin, thin, thin,
                square, square, square, square, square, square,
                wide, wide, wide, wide, wide,
                pltpu.VMEM((slots, size, 1, width), jnp.float32),
                dma((9,)),
                dma((slots,)),
                dma((3, slots)),
                dma((3, slots)),
                dma((2,)),
                dma((2,)),
                dma((slots,)),
                dma((slots,)),
                dma((slots,)),
                dma((slots,)),
                dma((slots,)),
            ],
            compiler_params=pltpu.CompilerParams(
                collective_id=0,
                has_side_effects=True,
                vmem_limit_bytes=60 * 1024 * 1024,
            ),
            cost_estimate=pl.CostEstimate(
                flops=18 * slots * size * size * width,
                bytes_accessed=16 * slots * size * size,
                transcendentals=0,
            ),
        )(slot_layer.reshape(slots), inverses, couplings,
          rhs.reshape(flat), previous.reshape(flat))
        result = pl.pallas_call(
            move,
            out_shape=jax.ShapeDtypeStruct(result.shape, result.dtype),
            in_specs=[hbm],
            out_specs=hbm,
            scratch_shapes=[
                pltpu.VMEM(result.shape, result.dtype), dma((slots,)), dma((slots,)),
            ],
            compiler_params=pltpu.CompilerParams(vmem_limit_bytes=60 * 1024 * 1024),
        )(result)
        return result.reshape(1, 1, *flat)

    return jax.shard_map(
        local,
        mesh=mesh,
        in_specs=(
            P("sweep", "span", None, None, None),
            P(None, "sweep", "span", None, None, None),
            P("sweep", "span", None, None, None),
            P("sweep", "span", None, None, None),
            P("sweep", "span", None),
        ),
        out_specs=P("sweep", "span", None, None, None),
        check_vma=False,
    )
```
